512 devices in a mesh: dom: 128 (over x, y_lo, z), sub: 4 (over y_hi, core).
Axes of the slice: x: 4, y: 8 (y_hi: 2, y_lo: 4; y = y_hi * 4 + y_lo), z: 8, core: 2. Of those that a mesh axis runs over, the one named last changes fastest.
Arguments:
- left_emb: float32 [262144, 256], P(('dom', 'sub')), may hold values from -1.5 to 1.5
- left_state: float32 [262144], P(('dom', 'sub')), may hold values from 0.003 to 0.3
- right_emb: float32 [131072, 256], P(('dom', 'sub')), may hold values from -1.5 to 1.5
- right_state: float32 [131072], P(('dom', 'sub')), may hold values from 0.003 to 0.3
- rel_ops: bfloat16 [512, 256, 256], P('dom'), may hold values from -0.375 to 0.375
- left_ids: int32 [2, 262144], P(None, ('dom', 'sub')), may hold values from 0 to 511
- right_ids: int32 [2, 262144], P(None, ('dom', 'sub')), may hold values from 0 to 1023
- relations: int32 [2, 262144, 1], P(None, ('dom', 'sub')), may hold values from 0 to 511; in each aligned block of 512 rows (0 to 511, 512 to 1023, ..., all dimensions but the last counted through in order) at most 2 rows name the same one
- negatives: int32 [2, 1024, 1024], P(None, ('dom', 'sub')), may hold values from 0 to 1023
- live: int32 [2, 512], P(None, ('dom', 'sub')), may hold values from 128 to 512, as said below
Outputs:
- left_out: float32 [262144, 256], P(('dom', 'sub'))
- right_out: float32 [131072, 256], P(('dom', 'sub'))
- rel_grad: float32 [512, 256, 256], P('dom')
The draws below stay inside these ranges and needn't reach their ends.
Inputs may be any that keep to these rules, and one draw needn't show every extreme that they name: `relations`: in one device's 512 rows of a round no relation is named more than 2 times. In every round some device has all 512 edges live.
All inputs are finite; a program needn't handle non-finite values.
Results may differ from the reference program's by a relative error of at most 0.015.
Values may be sent and summed in bfloat16 or wider, within the bound.
A program may use at most 64 MiB of HBM per device.

```python
import math
import jax
import jax.numpy as jnp
import numpy as np
from jax import lax

D = 256
REL = 512
LDEV = 512
EDGES = 512
SPAN = 256
NNEG = 1024
ROUNDS = 2
MOST = 2
RB = 1024
CPD = 2
ALL_EDGES = 262144
ALL_SPANS = 1024
LEFT_ROWS = 262144
RIGHT_ROWS = 131072
N_DOM = 128
N_SUB = 4


def draw_live(key, part):
    key = jax.random.fold_in(key, 5)
    draw_key, spot_key = jax.random.split(key)
    devices_all = N_DOM * N_SUB
    counts = jax.random.randint(draw_key, (ROUNDS, devices_all), EDGES // 4, EDGES + 1)
    full_at = jax.random.randint(spot_key, (ROUNDS, 1), 0, devices_all)
    positions = jnp.arange(devices_all, dtype=jnp.int32)[None, :]
    return jnp.where(positions == full_at, EDGES, counts).astype(jnp.int32)


def touch_ends(values, stream_key, least, top_value):
    dims = values.shape
    place = [jax.random.randint(jax.random.fold_in(stream_key, axis), (), 0, dims[axis]) for axis in range(len(dims))]
    values = values.at[tuple(place)].set(least)
    longest = dims.index(max(dims))
    place[longest] = (place[longest] + 1) % dims[longest]
    return values.at[tuple(place)].set(top_value)


def shard_levels(key, extent, shards, least, top_value):
    def one(axis_at, shards_of):
        heights = jax.random.uniform(jax.random.fold_in(jax.random.fold_in(key, 6), axis_at), (shards_of,), jnp.float32, least / len(shards), top_value / len(shards))
        return jnp.repeat(jnp.exp(heights), extent[axis_at] // shards_of).reshape((-1,) + (1,) * (len(extent) - axis_at - 1))

    factor_of = one(*shards[0])
    for cut in shards[1:]:
        factor_of = factor_of * one(*cut)
    return factor_of


def assign_block(stream_key, own, number, rows, amount, top, reach, slope):
    ranking = jax.random.permutation(stream_key, amount)
    heavy_load, usual = shares(amount, rows * top, reach, slope, True), shares(amount, rows * top, reach, slope, False)
    places = jnp.arange(amount)

    def named(sizes, turn):
        used = int((sizes > 0).sum())
        fixed = max(1, used // 4)
        moved = fixed + (places - fixed + turn * (used - fixed)) % max(1, amount - fixed)
        return jnp.zeros((amount,), jnp.int32).at[ranking[jnp.where(places < fixed, places, moved)]].set(jnp.asarray(sizes, jnp.int32))

    sizes = jnp.where(number % 4 == 0, named(heavy_load, number // 4), named(usual, number - number // 4 - 1))
    mixed = jax.random.permutation(jax.random.fold_in(own, 3), amount)
    source_of, receiver = mixed[0:amount // 2 * 2:2], mixed[1:amount // 2 * 2:2]
    slack = jnp.minimum(sizes[source_of] - 1, reach - sizes[receiver]) // 2
    slack = jnp.where((source_of == ranking[0]) | (receiver == ranking[0]) | (sizes[receiver] == 0), 0, jnp.maximum(slack, 0))
    moved = jax.random.randint(jax.random.fold_in(own, 4), (amount // 2,), 0, 1 << 20) % (slack + 1)
    sizes = sizes.at[source_of].add(-moved).at[receiver].add(moved)
    members = jnp.searchsorted(jnp.cumsum(sizes), jnp.arange(rows * top), side="right").astype(jnp.int32)
    table = members.reshape(top, rows).T
    table = table[jax.random.permutation(jax.random.fold_in(own, 1), rows)]
    turn = jax.random.randint(jax.random.fold_in(own, 2), (rows, 1), 0, top)
    return jnp.take_along_axis(table, (jnp.arange(top)[None, :] + turn) % top, axis=1)


def shares(amount, total, reach, lean, full):
    portions = [(1 << 20) // math.isqrt(grade ** lean) + 1 for grade in range(1, amount + 1)]
    largest = reach if full else min(reach, max(-(-total // amount), total * portions[0] // sum(portions)))
    least = 1 if total - largest >= amount - 1 else 0
    given, spare = [largest] + [least] * (amount - 1), total - largest - least * (amount - 1)
    while spare > 0:
        candidates = [i for i in range(1, amount) if given[i] < largest] or [i for i in range(1, amount) if given[i] < reach]
        pool, remaining = sum([portions[i] for i in candidates]), spare
        for i in candidates:
            extra = min(reach - given[i], max(1, remaining * portions[i] // pool), spare)
            given[i] = given[i] + extra
            spare = spare - extra
    return np.array(given)


def gaussian(stream_key, dims, deviation, limit, cuts=(), kind=jnp.bfloat16):
    values = deviation * jax.random.normal(stream_key, dims, jnp.float32)
    if cuts:
        values = values * shard_levels(stream_key, dims, cuts, -0.22, 0.18)
    return jnp.clip(values, -limit, limit).astype(kind)


def setup_inputs(seed: int = 0) -> dict:
    key_of = jax.random.split(jax.random.key(seed), 11)
    left_emb = gaussian(key_of[0], (LEFT_ROWS, D), 0.25, 1.5, ((0, 512),), jnp.float32)
    left_state = jnp.clip(jnp.exp(math.log(0.3) - 4.6051702 * jax.random.uniform(key_of[1], (LEFT_ROWS,), jnp.float32) ** shard_levels(key_of[1], (LEFT_ROWS,), ((0, 512),), -0.2, 0.2)), 0.003, 0.3)
    right_emb = gaussian(key_of[2], (RIGHT_ROWS, D), 0.25, 1.5, ((0, 512),), jnp.float32)
    right_state = jnp.clip(jnp.exp(math.log(0.3) - 4.6051702 * jax.random.uniform(key_of[3], (RIGHT_ROWS,), jnp.float32) ** shard_levels(key_of[3], (RIGHT_ROWS,), ((0, 512),), -0.2, 0.2)), 0.003, 0.3)
    rel_ops = gaussian(key_of[4], (REL, D, D), D ** -0.5, 0.375, ((0, 128),))
    left_ids = touch_ends(jax.random.randint(key_of[5], (ROUNDS, ALL_EDGES), 0, LDEV), jax.random.fold_in(key_of[5], 1), 0, LDEV - 1).astype(jnp.int32)
    right_ids = touch_ends(jax.random.randint(key_of[6], (ROUNDS, ALL_EDGES), 0, RB), jax.random.fold_in(key_of[6], 1), 0, RB - 1).astype(jnp.int32)
    relations_keys = jax.random.split(jax.random.fold_in(key_of[7], 1), ROUNDS * ALL_EDGES // EDGES)
    relations_turns = jax.random.permutation(jax.random.fold_in(key_of[7], 3), ROUNDS * ALL_EDGES // EDGES)
    relations = jax.vmap(lambda own, number: assign_block(jax.random.fold_in(key_of[7], 2), own, number, EDGES, REL, 1, MOST, 2))(relations_keys, relations_turns).reshape((ROUNDS, ALL_EDGES, 1))
    negatives = touch_ends(jax.random.randint(key_of[8], (ROUNDS, ALL_SPANS, NNEG), 0, RB), jax.random.fold_in(key_of[8], 1), 0, RB - 1).astype(jnp.int32)
    live = draw_live(jax.random.fold_in(key_of[10], 71), 0)
    return dict(left_emb=left_emb, left_state=left_state, right_emb=right_emb, right_state=right_state, rel_ops=rel_ops, left_ids=left_ids, right_ids=right_ids, relations=relations, negatives=negatives, live=live)


LEARNING_RATE = 0.1
STABILIZER = 1e-06

def adagrad(embedding, state, gradient):
    new_state = state + lax.optimization_barrier(jnp.mean(gradient * gradient, axis=1))
    step_size = LEARNING_RATE / (jnp.sqrt(new_state) + STABILIZER)
    return (embedding - step_size[:, None] * gradient, new_state)

def sorted_layout(relation_ids):
    count = relation_ids.shape[0]
    order = jnp.argsort(relation_ids, stable=True).astype(jnp.int32)
    totals = jax.ops.segment_sum(jnp.ones((count,), jnp.int32), relation_ids, num_segments=REL)
    starts = (jnp.cumsum(totals) - totals).astype(jnp.int32)
    return (order, totals, starts)

def transform(rows, relation_ids, mats, flip):
    count = rows.shape[0]
    window = N_DOM * N_SUB * MOST
    order, totals, starts = sorted_layout(relation_ids)
    padded = jnp.concatenate([rows[order], jnp.zeros((window, D), rows.dtype)], axis=0)

    def visit(accum, index):
        start = starts[index]
        piece = lax.dynamic_slice_in_dim(padded, start, window, 0)
        matrix = mats[index].T if flip else mats[index]
        product = jnp.dot(piece, matrix, preferred_element_type=jnp.float32)
        valid = (jnp.arange(window, dtype=jnp.int32) < totals[index])[:, None]
        current = lax.dynamic_slice_in_dim(accum, start, window, 0)
        accum = lax.dynamic_update_slice_in_dim(accum, current + jnp.where(valid, product, 0.0), start, 0)
        return (accum, None)
    accum, unused = lax.scan(visit, jnp.zeros((count + window, D), jnp.float32), jnp.arange(REL, dtype=jnp.int32))
    return jnp.zeros((count, D), jnp.float32).at[order].set(accum[:count])

def relation_grads(inputs, grads, relation_ids):
    window = N_DOM * N_SUB * MOST
    order, totals, starts = sorted_layout(relation_ids)
    padded_in = jnp.concatenate([inputs[order], jnp.zeros((window, D), inputs.dtype)], axis=0)
    padded_gr = jnp.concatenate([grads[order], jnp.zeros((window, D), grads.dtype)], axis=0)

    def visit(carry, index):
        start = starts[index]
        piece_in = lax.dynamic_slice_in_dim(padded_in, start, window, 0)
        piece_gr = lax.dynamic_slice_in_dim(padded_gr, start, window, 0)
        valid = (jnp.arange(window, dtype=jnp.int32) < totals[index])[:, None]
        piece_gr = jnp.where(valid, piece_gr, jnp.zeros_like(piece_gr))
        return (carry, jnp.dot(piece_in.T, piece_gr, preferred_element_type=jnp.float32))
    unused, result = lax.scan(visit, 0, jnp.arange(REL, dtype=jnp.int32))
    return result

def reference(left_emb, left_state, right_emb, right_state, rel_ops, left_ids, right_ids, relations, negatives, live):
    devices_all = N_DOM * N_SUB
    group_edges = N_SUB * EDGES
    group_spans = N_SUB * CPD
    edge_device = jnp.arange(devices_all * EDGES, dtype=jnp.int32) // EDGES
    left_cur, left_st = (left_emb, left_state)
    right_cur, right_st = (right_emb, right_state)
    rel_total = jnp.zeros((REL, D, D), jnp.float32)
    for bucket in range(ROUNDS):
        relation_ids = relations[bucket, :, 0]
        left_index = edge_device * LDEV + left_ids[bucket]
        gathered = left_cur[left_index].astype(jnp.bfloat16)
        mapped = transform(gathered, relation_ids, rel_ops, False).astype(jnp.bfloat16)
        block_of = ((jnp.arange(N_DOM, dtype=jnp.int32) - bucket) % N_DOM).astype(jnp.int32)
        right_blocks = right_cur.reshape(N_DOM, RB, D).astype(jnp.bfloat16)
        live_mask = (jnp.arange(EDGES, dtype=jnp.int32)[None, :] < live[bucket][:, None]).astype(jnp.float32)
        live_mask = live_mask.reshape(N_DOM, group_edges)
        right_now = right_ids[bucket]
        neg_now = negatives[bucket]

        def score_group(index):
            rows = right_blocks[block_of[index]]
            group = lax.dynamic_slice_in_dim(mapped, index * group_edges, group_edges, 0)
            pos_ids = lax.dynamic_slice_in_dim(right_now, index * group_edges, group_edges, 0)
            neg_ids = lax.dynamic_slice_in_dim(neg_now, index * group_spans, group_spans, 0)
            weights_live = live_mask[index]
            pos_rows = rows[pos_ids]
            neg_rows = rows[neg_ids]
            positive = lax.optimization_barrier(jnp.sum(group.astype(jnp.float32) * pos_rows.astype(jnp.float32), axis=1))
            blocks = group.reshape(group_spans, SPAN, D)
            scores = jnp.einsum('cid,cjd->cij', blocks.astype(jnp.float32), neg_rows.astype(jnp.float32))
            pos_weight = -jax.nn.sigmoid(-positive) * weights_live
            neg_weight = (jax.nn.sigmoid(scores) * weights_live.reshape(group_spans, SPAN, 1) / NNEG).astype(jnp.bfloat16)
            grad_mapped = pos_weight[:, None] * pos_rows.astype(jnp.float32) + jnp.einsum('cij,cjd->cid', neg_weight.astype(jnp.float32), neg_rows.astype(jnp.float32)).reshape(group_edges, D)
            grad_neg = jnp.einsum('cij,cid->cjd', neg_weight.astype(jnp.float32), blocks.astype(jnp.float32))
            pos_term = pos_weight[:, None] * group.astype(jnp.float32)

            def one_sub(pos_index, pos_part, neg_index, neg_part):
                return jnp.zeros((RB, D), jnp.float32).at[pos_index].add(pos_part).at[neg_index].add(neg_part)
            partial_value = jax.vmap(one_sub)(pos_ids.reshape(N_SUB, EDGES), pos_term.reshape(N_SUB, EDGES, D), neg_ids.reshape(N_SUB, CPD * NNEG), grad_neg.reshape(N_SUB, CPD * NNEG, D))
            rounded = lax.optimization_barrier(partial_value.astype(jnp.bfloat16))
            return (grad_mapped, lax.optimization_barrier(jnp.sum(rounded.astype(jnp.float32), axis=0)))
        grad_mapped, block_grads = lax.map(score_group, jnp.arange(N_DOM, dtype=jnp.int32))
        grad_mapped = grad_mapped.reshape(devices_all * EDGES, D).astype(jnp.bfloat16)
        input_grad = transform(grad_mapped, relation_ids, rel_ops, True).astype(jnp.bfloat16)
        rel_total = rel_total + relation_grads(gathered, grad_mapped, relation_ids)
        left_grad = jnp.zeros((devices_all * LDEV, D), jnp.float32).at[left_index].add(input_grad.astype(jnp.float32))
        left_cur, left_st = adagrad(left_cur, left_st, left_grad)
        right_grad = jnp.roll(block_grads, -bucket, axis=0).reshape(N_DOM * RB, D)
        right_cur, right_st = adagrad(right_cur, right_st, right_grad)
    right_out = jnp.roll(right_cur.reshape(N_DOM, RB, D), ROUNDS - 1, axis=0).reshape(N_DOM * RB, D)
    return (left_cur, right_out, rel_total)
```

```python
import jax
import jax.numpy as jnp
from jax import lax
from jax.experimental import pallas as pl
from jax.experimental.pallas import tpu as pltpu
from jax.sharding import PartitionSpec as P

LEARNING_RATE = 0.1
STABILIZER = 1e-06
MESH = pl.DeviceIdType.MESH
F32 = jnp.float32
BF16 = jnp.bfloat16
NX, NY, NZ = 4, 4, 8
DOM = NX * NY * NZ
WIDTH = 256
EDGES = 512
SLOTS = 1024
ROWS = 512
BLOCK = 1024
PART = 256
NEG = 1024


def dot(a, b):
    return lax.dot_general(a, b, (((1,), (0,)), ((), ())), preferred_element_type=F32)


def dot_bt(a, b):
    return lax.dot_general(a, b, (((1,), (1,)), ((), ())), preferred_element_type=F32)


def dot_at(a, b):
    return lax.dot_general(a, b, (((0,), (0,)), ((), ())), preferred_element_type=F32)


def iota(shape, dim):
    return lax.broadcasted_iota(jnp.int32, shape, dim)


def onehot(hit):
    return jnp.where(hit, 1.0, 0.0).astype(BF16)


def pack(rows):
    n = rows.shape[0] // 8
    low = rows[:, :128].reshape(n, 8, 128)
    high = rows[:, 128:].reshape(n, 8, 128)
    return jnp.concatenate([low, high], axis=1).astype(BF16)


def unpack(chunks):
    n = chunks.shape[0]
    wide = chunks.astype(F32)
    low = wide[:, :8].reshape(n * 8, 128)
    high = wide[:, 8:].reshape(n * 8, 128)
    return jnp.concatenate([low, high], axis=1)


def place():
    me = lax.axis_index("dom")
    sub = lax.axis_index("sub")
    return me // (NY * NZ), (me // NZ) % NY, me % NZ, sub // 2, sub % 2


def each_partner(visit):
    mx, my, mz, yh, core = place()
    for dy in range(NY):
        qy = lax.rem(my + dy, NY)
        if dy == 0:
            flip = 0
        elif dy == 1:
            flip = jnp.where(my == NY - 1, 1, 0)
        elif dy == NY - 1:
            flip = jnp.where(my == 0, 1, 0)
        else:
            flip = core
        sub = lax.rem(yh + flip, 2) * 2 + core

        def plane(dx, first):
            base = (lax.rem(mx + dx, NX) * NY + qy) * NZ
            for dz in range(NZ):
                if not (first and dz == 0):
                    q = base + lax.rem(mz + dz, NZ)
                    visit(q, (q, sub))

        def body(dx, carry):
            plane(dx, False)
            return carry

        if dy == 0:
            plane(0, True)
            lax.fori_loop(1, NX, body, 0)
        else:
            lax.fori_loop(0, NX, body, 0)


def kernel(
    left_ref, lstate_ref, right_ref, rstate_ref, rel_ref, lids_ref, rids_ref, rels_ref, negs_ref, live_ref,
    left_out, right_out, rel_out,
    send, recv, to_slot, from_slot, row_slot, slot_row, ids, counts, rel_t, inbox, masked, moved, edge_grad, weights,
    blk, part, part_in, lstate, rstate, shift_e, shift_e_in, shift_s, shift_s_in, rel_acc, rel_send, rel_in,
    a2a_s, a2a_r, gat_s, gat_r, red_s, red_r, shf_s, shf_r, rel_s, rel_r,
):
    me = lax.axis_index("dom")
    sub = lax.axis_index("sub")
    core = lax.rem(sub, 2)
    following = (lax.rem(me + 1, DOM), sub)
    previous = (lax.rem(me + DOM - 1, DOM), sub)
    relatives = [(me, lax.rem(sub // 2 + o // 2, 2) * 2 + lax.rem(core + o % 2, 2)) for o in (1, 2, 3)]

    barrier = pltpu.get_barrier_semaphore()

    def greet(q, device):
        pl.semaphore_signal(barrier, inc=1, device_id=device, device_id_type=MESH)

    each_partner(greet)
    for device in relatives + [following, previous]:
        greet(None, device)

    def remote(src, dst, send_sem, recv_sem, device):
        return pltpu.make_async_remote_copy(
            src_ref=src, dst_ref=dst, send_sem=send_sem, recv_sem=recv_sem, device_id=device, device_id_type=MESH
        )

    def blocks(count, body):
        def step(i, carry):
            body(i)
            return carry

        lax.fori_loop(0, count, step, 0)

    def exchange(k):
        def start(q, device):
            remote(send.at[k % 2, q], recv.at[k, me], a2a_s.at[k], a2a_r.at[k], device).start()

        each_partner(start)
        recv[k, me] = send[k % 2, me]

    def sent(k):
        most = send.at[k % 2, pl.ds(0, DOM - 1)]
        pltpu.make_async_copy(most, most, a2a_s.at[k]).wait()

    def arrived(k):
        most = recv.at[k, pl.ds(0, DOM - 1)]
        pltpu.make_async_copy(most, most, a2a_r.at[k]).wait()

    rows = jnp.concatenate(
        [rels_ref[...].astype(F32), lids_ref[...].astype(F32), rids_ref[...].astype(F32), lstate_ref[...],
         jnp.zeros((1, EDGES), F32)], axis=0)
    ids[...] = jnp.transpose(rows)
    lstate[...] = ids[:, 6:7]
    rstate[...] = jnp.transpose(jnp.broadcast_to(rstate_ref[...], (8, PART)))[:, 0:1]

    def index_work(r, stage):
        if stage == 0:
            rel_row = rels_ref[r : r + 1, :].astype(F32)
            rel_col = ids[:, r : r + 1]
            same = rel_row == rel_col
            lane, line = iota((EDGES, EDGES), 1), iota((EDGES, EDGES), 0)
            row_rank = jnp.sum(jnp.where(same & (line < lane), 1.0, 0.0), axis=0, keepdims=True)
            col_rank = jnp.sum(jnp.where(same & (lane < line), 1.0, 0.0), axis=1, keepdims=True)
            ids[:, 7:8] = 2.0 * rel_col + col_rank
            row_ids = (2.0 * rel_row + row_rank).astype(jnp.int32)
            gather = onehot(iota((EDGES, ROWS), 1) == ids[:, 2 + r : 3 + r].astype(jnp.int32))

            def fill(i):
                place_of = onehot(iota((256, EDGES), 0) + i * 256 == row_ids)
                to_slot[r, pl.ds(i * 256, 256), :] = place_of
                slot_row[r, pl.ds(i * 256, 256), :] = dot(place_of, gather).astype(BF16)

            blocks(4, fill)
        else:
            slot = ids[:, 7:8].astype(jnp.int32)
            for i in range(4):
                from_slot[r, :, i * 256 : (i + 1) * 256] = onehot(iota((EDGES, 256), 1) + i * 256 == slot)
            scatter = onehot(iota((ROWS, EDGES), 0) == lids_ref[r : r + 1, :])
            for i in range(4):
                row_slot[r, :, i * 256 : (i + 1) * 256] = dot(scatter, from_slot[r, :, i * 256 : (i + 1) * 256]).astype(BF16)
            for c in range(2):
                named = negs_ref[r, c : c + 1, :]
                high = onehot(iota((16, NEG), 0) == named // 128)
                low = onehot(iota((128, NEG), 0) == named % 128)
                tally = dot_bt(high, low)
                counts[2 * r + c : 2 * r + c + 1, :] = (
                    jnp.concatenate([tally[i : i + 1, :] for i in range(8)], axis=1) * (1.0 / NEG))

    def fill_outbox(k, table, r, values):
        def fill(i):
            send[k % 2, pl.ds(i * 32, 32)] = pack(dot(table[r, pl.ds(i * 256, 256), :], values))

        blocks(4, fill)

    def keep(o):
        return (iota((256, WIDTH), 0) % 8) // 2 == o

    def adagrad(value, state, gradient):
        state = state + jnp.mean(gradient * gradient, axis=1, keepdims=True)
        return value - LEARNING_RATE / (jnp.sqrt(state) + STABILIZER) * gradient, state

    def gather_block(r):
        for o in range(3):
            remote(blk.at[r, sub], blk.at[r, sub], gat_s.at[r, o], gat_r.at[r, o], relatives[o]).start()

    index_work(0, 0)
    left_out[...] = left_ref[...]
    fill_outbox(0, slot_row, 0, left_out[...].astype(BF16))
    blk[0, sub] = right_ref[...].astype(BF16)
    pl.semaphore_wait(barrier, DOM - 1 + 5)

    for r in range(2):
        k = 4 * r
        exchange(k)
        if r == 0:
            gather_block(0)
            index_work(0, 1)
            for o in range(4):
                rel_t[o] = jnp.transpose(rel_ref[o].astype(F32)).astype(BF16)
            right_now = right_ref
        else:
            for copy in shifts:
                copy.wait_recv()
            blk[1, sub] = shift_e_in[...]
            gather_block(1)
            rstate[...] = jnp.transpose(shift_s_in[...])[:, 0:1]
            right_now = shift_e_in
        arrived(k)
        if r == 1:
            sent(k - 1)

        def forward(i):
            row = unpack(recv[k, pl.ds(i * 32, 32)])
            inbox[r, pl.ds(i * 256, 256), :] = row.astype(BF16)
            mapped = sum(dot(jnp.where(keep(o), row, 0.0).astype(BF16), rel_ref[o]) for o in range(4))
            send[(k + 1) % 2, pl.ds(i * 32, 32)] = pack(mapped)

        blocks(4, forward)
        exchange(k + 1)
        if r == 0:
            index_work(1, 0)
            index_work(1, 1)
        arrived(k + 1)

        def settle(i):
            row = unpack(recv[k + 1, pl.ds(i * 32, 32)])
            inbox[2, pl.ds(i * 256, 256), :] = row.astype(BF16)

        blocks(4, settle)
        moved[...] = dot(from_slot[r], inbox[2]).astype(BF16)
        for o in range(3):
            remote(blk.at[r, sub], blk.at[r, sub], gat_s.at[r, o], gat_r.at[r, o], relatives[o]).wait()

        live = live_ref[r : r + 1, :]

        def score(i):
            at = pl.ds(i * 128, 128)
            y = moved[at, :]
            scores = jnp.concatenate([dot_bt(y, blk[r, j]) for j in range(4)], axis=1)
            mask = jnp.where(iota((128, 1), 0) + i * 128 < live, 1.0, 0.0)
            named = iota((128, BLOCK), 1) == ids[at, 4 + r : 5 + r].astype(jnp.int32)
            positive = jnp.sum(jnp.where(named, scores, 0.0), axis=1, keepdims=True)
            pull = -jax.nn.sigmoid(-positive) * mask
            push = jax.nn.sigmoid(scores) * counts[pl.ds(2 * r + i // 2, 1), :] * mask
            weight = (push + jnp.where(named, pull, 0.0)).astype(BF16)
            weights[at, :] = weight
            grad = sum(dot(weight[:, j * 256 : (j + 1) * 256], blk[r, j]) for j in range(4))
            edge_grad[at, :] = grad.astype(BF16)

        blocks(4, score)
        sent(k)
        fill_outbox(k + 2, to_slot, r, edge_grad[...])
        exchange(k + 2)
        for j in range(4):
            part[r, j] = dot_at(weights[:, j * 256 : (j + 1) * 256], moved[...]).astype(BF16)
        for o in range(3):
            remote(part.at[r, relatives[o][1]], part_in.at[r, o], red_s.at[r, o], red_r.at[r, o], relatives[o]).start()
        arrived(k + 2)
        sent(k + 1)

        def backward(i):
            row = unpack(recv[k + 2, pl.ds(i * 32, 32)])
            total = jnp.zeros((256, WIDTH), F32)
            for o in range(4):
                kept = jnp.where(keep(o), row, 0.0).astype(BF16)
                masked[o, pl.ds(i * 256, 256), :] = kept
                total = total + dot(kept, rel_t[o])
            send[(k + 3) % 2, pl.ds(i * 32, 32)] = pack(total)

        blocks(4, backward)
        exchange(k + 3)
        for o in range(4):
            term = dot_at(inbox[r], masked[o])
            rel_acc[o] = term if r == 0 else rel_acc[o] + term
        if r == 1:
            for o in range(4):
                rel_send[0, o] = rel_acc[o].astype(BF16)
            pair = [remote(rel_send.at[0, pl.ds(2 - 2 * core, 2)], rel_in.at[0], rel_s.at[0], rel_r.at[0], relatives[0])]
            pair[0].start()
        for o in range(3):
            remote(part.at[r, relatives[o][1]], part_in.at[r, o], red_s.at[r, o], red_r.at[r, o], relatives[o]).wait()
        gradient = part[r, sub].astype(F32)
        for o in range(3):
            gradient = gradient + part_in[r, o].astype(F32)
        value, state = adagrad(right_now[...].astype(F32), rstate[...], gradient)
        if r == 0:
            shift_e[...] = value.astype(BF16)
            shift_s[...] = jnp.transpose(jnp.broadcast_to(state, (PART, 128)))[0:8, :]
            shifts = [
                remote(shift_e, shift_e_in, shf_s.at[0], shf_r.at[0], following),
                remote(shift_s, shift_s_in, shf_s.at[1], shf_r.at[1], following),
            ]
            for copy in shifts:
                copy.start()
        else:
            right_out[...] = value
            pair[0].wait()
            for o in range(2):
                rel_send[1, o] = (rel_acc[2 * core + o] + rel_in[0, o].astype(F32)).astype(BF16)
            across = remote(rel_send.at[1, pl.ds(0, 2)], rel_in.at[1], rel_s.at[1], rel_r.at[1], relatives[1])
            across.start()
        arrived(k + 3)
        sent(k + 2)

        def settle_back(i):
            row = unpack(recv[k + 3, pl.ds(i * 32, 32)])
            inbox[2, pl.ds(i * 256, 256), :] = row.astype(BF16)

        blocks(4, settle_back)

        def update(i):
            at = pl.ds(i * 128, 128)
            value, state = adagrad(left_out[at, :], lstate[at, :], dot(row_slot[r, at, :], inbox[2]))
            left_out[at, :] = value
            lstate[at, :] = state

        blocks(4, update)
        if r == 0:
            fill_outbox(k + 4, slot_row, 1, left_out[...].astype(BF16))
    across.wait()
    for o in range(2):
        rel_send[2, o] = (rel_send[1, o].astype(F32) + rel_in[1, o].astype(F32)).astype(BF16)
    back = remote(rel_send.at[2, pl.ds(0, 2)], rel_in.at[2], rel_s.at[2], rel_r.at[2], relatives[0])
    back.start()
    for o in range(2):
        rel_out[2 * core + o] = rel_send[2, o].astype(F32)
    back.wait()
    for o in range(2):
        rel_out[2 - 2 * core + o] = rel_in[2, o].astype(F32)
    for copy in shifts:
        copy.wait_send()
    sent(7)


def per_device(left_emb, left_state, right_emb, right_state, rel_ops, left_ids, right_ids, relations, negatives, live):
    vmem = pltpu.VMEM
    dma = pltpu.SemaphoreType.DMA
    whole = pl.BlockSpec(memory_space=pltpu.VMEM)
    return pl.pallas_call(
        kernel,
        out_shape=(
            jax.ShapeDtypeStruct((ROWS, WIDTH), F32),
            jax.ShapeDtypeStruct((PART, WIDTH), F32),
            jax.ShapeDtypeStruct((4, WIDTH, WIDTH), F32),
        ),
        in_specs=[whole] * 10,
        out_specs=[whole] * 3,
        scratch_shapes=[
            vmem((2, DOM, 16, 128), BF16),
            vmem((8, DOM, 16, 128), BF16),
            vmem((2, SLOTS, EDGES), BF16),
            vmem((2, EDGES, SLOTS), BF16),
            vmem((2, ROWS, SLOTS), BF16),
            vmem((2, SLOTS, ROWS), BF16),
            vmem((EDGES, 8), F32),
            vmem((8, BLOCK), F32),
            vmem((4, WIDTH, WIDTH), BF16),
            vmem((3, SLOTS, WIDTH), BF16),
            vmem((4, SLOTS, WIDTH), BF16),
            vmem((EDGES, WIDTH), BF16),
            vmem((EDGES, WIDTH), BF16),
            vmem((EDGES, BLOCK), BF16),
            vmem((2, 4, PART, WIDTH), BF16),
            vmem((2, 4, PART, WIDTH), BF16),
            vmem((2, 3, PART, WIDTH), BF16),
            vmem((ROWS, 1), F32),
            vmem((PART, 1), F32),
            vmem((PART, WIDTH), BF16),
            vmem((PART, WIDTH), BF16),
            vmem((8, PART), F32),
            vmem((8, PART), F32),
            vmem((4, WIDTH, WIDTH), F32),
            vmem((3, 4, WIDTH, WIDTH), BF16),
            vmem((3, 2, WIDTH, WIDTH), BF16),
            dma((8,)), dma((8,)), dma((2, 3)), dma((2, 3)), dma((2, 3)), dma((2, 3)),
            dma((2,)), dma((2,)), dma((3,)), dma((3,)),
        ],
        compiler_params=pltpu.CompilerParams(collective_id=0, has_side_effects=True, vmem_limit_bytes=50 << 20),
    )(
        left_emb, left_state.reshape(1, -1), right_emb, right_state.reshape(1, -1), rel_ops, left_ids, right_ids,
        relations.reshape(2, -1), negatives, live,
    )


def solution(mesh):
    placed = (
        P(("dom", "sub"), None),
        P(("dom", "sub")),
        P(("dom", "sub"), None),
        P(("dom", "sub")),
        P("dom", None, None),
        P(None, ("dom", "sub")),
        P(None, ("dom", "sub")),
        P(None, ("dom", "sub"), None),
        P(None, ("dom", "sub"), None),
        P(None, ("dom", "sub")),
    )
    return jax.shard_map(
        per_device,
        mesh=mesh,
        in_specs=placed,
        out_specs=(P(("dom", "sub"), None), P(("dom", "sub"), None), P("dom", None, None)),
        check_vma=False,
    )
```

```python
import jax
import jax.numpy as jnp
from jax import lax
from jax.experimental import pallas as pl
from jax.experimental.pallas import tpu as pltpu
from jax.sharding import PartitionSpec as P

LEARNING_RATE = 0.1
STABILIZER = 1e-06
MESH = pl.DeviceIdType.MESH
F32 = jnp.float32
BF16 = jnp.bfloat16
NX, NY, NZ = 4, 4, 8
DOM = NX * NY * NZ
WIDTH = 256
EDGES = 512
SLOTS = 1024
ROWS = 512
BLOCK = 1024
PART = 256
NEG = 1024


def dot(a, b):
    return lax.dot_general(a, b, (((1,), (0,)), ((), ())), preferred_element_type=F32)


def dot_bt(a, b):
    return lax.dot_general(a, b, (((1,), (1,)), ((), ())), preferred_element_type=F32)


def dot_at(a, b):
    return lax.dot_general(a, b, (((0,), (0,)), ((), ())), preferred_element_type=F32)


def iota(shape, dim):
    return lax.broadcasted_iota(jnp.int32, shape, dim)


def onehot(hit):
    return jnp.where(hit, 1.0, 0.0).astype(BF16)


def pack(rows):
    n = rows.shape[0] // 8
    low = rows[:, :128].reshape(n, 8, 128)
    high = rows[:, 128:].reshape(n, 8, 128)
    return jnp.concatenate([low, high], axis=1).astype(BF16)


def unpack(chunks):
    n = chunks.shape[0]
    wide = chunks.astype(F32)
    low = wide[:, :8].reshape(n * 8, 128)
    high = wide[:, 8:].reshape(n * 8, 128)
    return jnp.concatenate([low, high], axis=1)


def place():
    me = lax.axis_index("dom")
    sub = lax.axis_index("sub")
    return me // (NY * NZ), (me // NZ) % NY, me % NZ, sub // 2, sub % 2


ALONG_Z = ((0, 0), (0, 1), (1, 0), (1, 1), (7, 0), (7, 1), (2, 0), (6, 0))
BACKWARD = (0, 1, 4, 5, 2, 3, 7, 6)


def each_partner(sign, dx, visit):
    mx, my, mz, yh, core = place()
    mine = (mx * NY + my) * NZ
    qx = lax.rem(mx + (dx if sign > 0 else NX - dx), NX)
    for dy in range(NY):
        qy = lax.rem(my + dy, NY)
        if dy == 0:
            flips = (0, 0)
        elif dy == 1:
            flips = (jnp.where(my == NY - 1, 1, 0),) * 2
        elif dy == NY - 1:
            flips = (jnp.where(my == 0, 1, 0),) * 2
        else:
            flips = (core, lax.rem(mx + qx, 2))
        base = (qx * NY + qy) * NZ
        for j, (dz, other_core) in enumerate(ALONG_Z):
            z = lax.rem(mz + dz, NZ)
            there = 1 - core if other_core else core
            sub = lax.rem(yh + flips[other_core], 2) * 2 + there
            owner = base + lax.rem(z + 4 * there, NZ)
            visit(owner, base + j, mine + BACKWARD[j], (base + z, sub), dy == 0 and j == 0)


def kernel(
    left_hbm, lstate_hbm, right_hbm, rstate_hbm, rel_hbm, lids_hbm, rids_hbm, rels_hbm, negs_hbm, live_hbm,
    left_out, right_out, rel_out,
    left_now, lstate_ref, right_now, rstate_ref, rel_now, lids_ref, rids_ref, rels_ref, negs_ref, live_ref,
    send, recv, to_slot, from_slot, row_slot, slot_row, ids, counts, rel_t, inbox, total, moved, edge_grad, weights,
    blk, part, part_in, half, half_in, lstate, rstate, shift_e, shift_e_in, shift_s, shift_s_in, rel_acc, rel_send, rel_in, rel_sum,
    a2a_s, a2a_r, gat_s, gat_r, red_s, red_r, shf_s, shf_r, rel_s, rel_r, sum_s, sum_r, swp_s, swp_r, load_s,
):
    me = lax.axis_index("dom")
    sub = lax.axis_index("sub")
    mx, my, mz, yh, core = place()
    across_z = (mx * NY + my) * NZ + lax.rem(mz + 4, NZ)
    home = jnp.where(core == 0, me, across_z)
    following = (lax.rem(me + 1, DOM), sub)
    previous = (lax.rem(me + DOM - 1, DOM), sub)
    relatives = [(me, lax.rem(sub // 2 + o // 2, 2) * 2 + lax.rem(core + o % 2, 2)) for o in (1, 2, 3)]

    sources = (left_hbm, lstate_hbm, right_hbm, rstate_hbm, rel_hbm, lids_hbm, rids_hbm, rels_hbm, negs_hbm, live_hbm)
    places = (left_now, lstate_ref, right_now, rstate_ref, rel_now, lids_ref, rids_ref, rels_ref, negs_ref, live_ref)
    copies = [pltpu.make_async_copy(src, dst, load_s.at[i]) for i, (src, dst) in enumerate(zip(sources, places))]
    for i in (7, 5, 6, 1, 3, 9, 0, 2, 8):
        copies[i].start()
    barrier = pltpu.get_barrier_semaphore()

    def greet(device):
        pl.semaphore_signal(barrier, inc=1, device_id=device, device_id_type=MESH)

    def planes(body):
        def step(dx, carry):
            body(dx)
            return carry

        lax.fori_loop(0, NX, step, 0)

    def greet_plane(dx):
        def visit(owner, other, there, device, first):
            if first:
                pl.when(dx != 0)(lambda: greet(device))
            else:
                greet(device)

        each_partner(1, dx, visit)

    planes(greet_plane)
    for device in relatives + [following, previous] + [(across_z, o) for o in range(4)]:
        greet(device)

    def remote(src, dst, send_sem, recv_sem, device):
        return pltpu.make_async_remote_copy(
            src_ref=src, dst_ref=dst, send_sem=send_sem, recv_sem=recv_sem, device_id=device, device_id_type=MESH
        )

    def blocks(count, body):
        def step(i, carry):
            body(i)
            return carry

        lax.fori_loop(0, count, step, 0)

    def plane_at(sign, dx):
        return lax.rem(mx + (dx if sign > 0 else NX - dx), NX)

    def send_plane(k, dx):
        outward = k % 2 == 0

        def visit(owner, other, there, device, first):
            chunk, landing = (owner, there) if outward else (other, home)
            copy = remote(send.at[k % 2, chunk], recv.at[k, landing], a2a_s.at[k], a2a_r.at[k, dx], device)
            if first:
                pl.when(dx != 0)(copy.start)

                @pl.when(dx == 0)
                def _():
                    pltpu.make_async_copy(send.at[k % 2, chunk], recv.at[k, landing], a2a_r.at[k, dx]).start()
            else:
                copy.start()

        each_partner(1 if outward else -1, dx, visit)

    def sent(k):
        most = send.at[k % 2, pl.ds(0, DOM - 1)]
        pltpu.make_async_copy(most, most, a2a_s.at[k]).wait()

    def arrived(k, dx):
        plane = recv.at[k, pl.ds(0, 32)]
        pltpu.make_async_copy(plane, plane, a2a_r.at[k, dx]).wait()
        return plane_at(-1 if k % 2 == 0 else 1, dx)

    for i in (1, 3, 5, 6, 7, 9):
        copies[i].wait()
    loads = [copies[i] for i in (0, 2, 8)]
    rows = jnp.concatenate(
        [rels_ref[0].astype(F32), rels_ref[1].astype(F32), lids_ref[...].astype(F32), rids_ref[...].astype(F32), lstate_ref[...],
         jnp.zeros((1, EDGES), F32)], axis=0)
    ids[...] = jnp.transpose(rows)
    lstate[...] = ids[:, 6:7]
    rstate[...] = jnp.transpose(jnp.broadcast_to(rstate_ref[...], (8, PART)))[:, 0:1]

    def index_work(r, stage):
        if stage == 0:
            rel_row = rels_ref[r].astype(F32)
            rel_col = ids[:, r : r + 1]
            same = rel_row == rel_col
            lane, line = iota((EDGES, EDGES), 1), iota((EDGES, EDGES), 0)
            row_rank = jnp.sum(jnp.where(same & (line < lane), 1.0, 0.0), axis=0, keepdims=True)
            col_rank = jnp.sum(jnp.where(same & (lane < line), 1.0, 0.0), axis=1, keepdims=True)
            ids[:, 7:8] = 2.0 * rel_col + col_rank
            row_ids = (2.0 * rel_row + row_rank).astype(jnp.int32)
            gather = onehot(iota((EDGES, ROWS), 1) == ids[:, 2 + r : 3 + r].astype(jnp.int32))

            def fill(i):
                place_of = onehot(iota((256, EDGES), 0) + i * 256 == row_ids)
                to_slot[r, i] = place_of
                slot_row[r, i] = dot(place_of, gather).astype(BF16)

            blocks(4, fill)
        else:
            slot = ids[:, 7:8].astype(jnp.int32)
            for i in range(4):
                from_slot[r, i] = onehot(iota((EDGES, 256), 1) + i * 256 == slot)
            scatter = onehot(iota((ROWS, EDGES), 0) == lids_ref[r : r + 1, :])
            for i in range(4):
                row_slot[r, i] = dot(scatter, from_slot[r, i]).astype(BF16)
            for c in range(2):
                named = negs_ref[r, c : c + 1, :]
                high = onehot(iota((16, NEG), 0) == named // 128)
                low = onehot(iota((128, NEG), 0) == named % 128)
                tally = dot_bt(high, low)
                counts[2 * r + c : 2 * r + c + 1, :] = (
                    jnp.concatenate([tally[i : i + 1, :] for i in range(8)], axis=1) * (1.0 / NEG))

    def send_rows(k, table, values):
        def step(dx):
            p = plane_at(1, dx)
            send[k % 2, pl.ds(p * 32, 32)] = pack(dot(table[p], values))
            send_plane(k, dx)

        planes(step)

    def keep(o):
        return (iota((256, WIDTH), 0) % 8) // 2 == o

    def adagrad(value, state, gradient):
        state = state + jnp.mean(gradient * gradient, axis=1, keepdims=True)
        return value - LEARNING_RATE / (jnp.sqrt(state) + STABILIZER) * gradient, state

    def block_copies(r):
        theirs = relatives[1][1]
        return [
            remote(blk.at[r, sub], blk.at[r, sub], gat_s.at[r, 0], gat_r.at[r, 0], relatives[0]),
            remote(blk.at[r, sub], blk.at[r, sub], gat_s.at[r, 1], gat_r.at[r, 1], relatives[1]),
            remote(blk.at[r, theirs], blk.at[r, theirs], gat_s.at[r, 2], gat_r.at[r, 2], relatives[0]),
        ]

    def gather_block(r):
        copies = block_copies(r)
        copies[1].start()
        copies[0].start()

    def pass_block_on(r):
        copies = block_copies(r)
        copies[1].wait_recv()
        copies[2].start()

    def block_ready(r):
        copies = block_copies(r)
        copies[0].wait()
        copies[1].wait_send()
        copies[2].wait()

    def sum_copies(r):
        return [
            remote(part.at[r, 1 - core], part_in.at[r], red_s.at[r, 0], red_r.at[r, 0], relatives[0]),
            remote(half.at[r], half_in.at[r], red_s.at[r, 1], red_r.at[r, 1], relatives[1]),
        ]

    def sum_across(r):
        copies = sum_copies(r)
        copies[0].wait()
        half[r] = (part[r, core, 1 - yh].astype(F32) + part_in[r, 1 - yh].astype(F32)).astype(BF16)
        copies[1].start()

    def right_update(r, value):
        sum_copies(r)[1].wait()
        gradient = part[r, core, yh].astype(F32) + part_in[r, yh].astype(F32) + half_in[r].astype(F32)
        return adagrad(value.astype(F32), rstate[...], gradient)

    index_work(0, 0)
    for copy in loads:
        copy.wait()
    left_bf = left_now[...].astype(BF16)
    blk[0, sub] = right_now[...].astype(BF16)
    pl.semaphore_wait(barrier, DOM - 1 + 9)
    swap = remote(rel_hbm, rel_now, swp_s, swp_r, (across_z, sub))
    pl.when(core == 1)(swap.start)
    pl.when(core == 0)(copies[4].start)
    rel_acc[...] = jnp.zeros((4, WIDTH, WIDTH), F32)

    for r in range(2):
        k = 4 * r
        send_rows(k, slot_row.at[r], left_bf)
        total[...] = jnp.zeros((EDGES, WIDTH), F32)
        if r == 0:
            gather_block(0)
            index_work(0, 1)
            pl.when(core == 1)(swap.wait)
            pl.when(core == 0)(copies[4].wait)
        else:
            value, state = right_update(0, right_now[...])
            shift_e[...] = value.astype(BF16)
            shift_s[...] = jnp.transpose(jnp.broadcast_to(state, (PART, 128)))[0:8, :]
            shifts = [
                remote(shift_e, shift_e_in, shf_s.at[0], shf_r.at[0], following),
                remote(shift_s, shift_s_in, shf_s.at[1], shf_r.at[1], following),
            ]
            for copy in shifts:
                copy.start()
            sent(k - 1)

        def forward(dx):
            p = arrived(k, dx)
            row = unpack(recv[k, pl.ds(p * 32, 32)])
            inbox[r, p] = row.astype(BF16)
            mapped = sum(dot(jnp.where(keep(o), row, 0.0).astype(BF16), rel_now[o]) for o in range(4))
            send[(k + 1) % 2, pl.ds(p * 32, 32)] = pack(mapped)
            send_plane(k + 1, dx)

        planes(forward)
        if r == 0:
            for o in range(4):
                rel_t[o] = jnp.transpose(rel_now[o].astype(F32)).astype(BF16)
            index_work(1, 0)
            index_work(1, 1)
        else:
            for copy in shifts:
                copy.wait_recv()
            blk[1, sub] = shift_e_in[...]
            gather_block(1)
            rstate[...] = jnp.transpose(shift_s_in[...])[:, 0:1]
        if r == 0:
            pass_block_on(r)

        def settle(dx):
            if r == 1:
                pl.when(dx == NX - 1)(lambda: pass_block_on(1))
            p = arrived(k + 1, dx)
            total[...] += dot(from_slot[r, p], unpack(recv[k + 1, pl.ds(p * 32, 32)]).astype(BF16))

        planes(settle)
        moved[...] = total[...].astype(BF16)
        total[...] = jnp.zeros((EDGES, WIDTH), F32)
        block_ready(r)

        live = live_ref[:, r : r + 1]

        def score(i):
            at = pl.ds(i * 128, 128)
            y = moved[at, :]
            scores = jnp.concatenate([dot_bt(y, blk[r, j]) for j in range(4)], axis=1)
            mask = jnp.where(iota((128, 1), 0) + i * 128 < live, 1.0, 0.0)
            named = iota((128, BLOCK), 1) == ids[at, 4 + r : 5 + r].astype(jnp.int32)
            positive = jnp.sum(jnp.where(named, scores, 0.0), axis=1, keepdims=True)
            pull = -jax.nn.sigmoid(-positive) * mask
            push = jax.nn.sigmoid(scores) * counts[pl.ds(2 * r + i // 2, 1), :] * mask
            weight = (push + jnp.where(named, pull, 0.0)).astype(BF16)
            weights[at, :] = weight
            grad = sum(dot(weight[:, j * 256 : (j + 1) * 256], blk[r, j]) for j in range(4))
            edge_grad[at, :] = grad.astype(BF16)

        blocks(4, score)
        sent(k)
        send_rows(k + 2, to_slot.at[r], edge_grad[...])
        for j in range(4):
            part[r, j % 2, j // 2] = dot_at(weights[:, j * 256 : (j + 1) * 256], moved[...]).astype(BF16)
        sum_copies(r)[0].start()
        sent(k + 1)

        def backward(dx):
            pl.when(dx == 1)(lambda: sum_across(r))
            p = arrived(k + 2, dx)
            row = unpack(recv[k + 2, pl.ds(p * 32, 32)])
            kept = [jnp.where(keep(o), row, 0.0).astype(BF16) for o in range(4)]
            send[(k + 3) % 2, pl.ds(p * 32, 32)] = pack(sum(dot(kept[o], rel_t[o]) for o in range(4)))
            send_plane(k + 3, dx)
            for o in range(4):
                rel_acc[o] += dot_at(inbox[r, p], kept[o])

        planes(backward)
        if r == 1:
            for o in range(4):
                rel_send[o] = rel_acc[o].astype(BF16)
                stays = (core == 0) & (sub == o)
                pl.when(stays)(pltpu.make_async_copy(rel_send.at[o], rel_in.at[sub], rel_r.at[sub]).start)
                pl.when(jnp.logical_not(stays))(
                    remote(rel_send.at[o], rel_in.at[sub], rel_s.at[o], rel_r.at[sub], (home, o)).start)

        def settle_back(dx):
            p = arrived(k + 3, dx)
            total[...] += dot(row_slot[r, p], unpack(recv[k + 3, pl.ds(p * 32, 32)]).astype(BF16))

        planes(settle_back)
        sent(k + 2)
        value, state = adagrad(left_now[...], lstate[...], total[...])
        if r == 0:
            left_now[...] = value
            lstate[...] = state
            left_bf = value.astype(BF16)
        else:
            left_out[...] = value
            value, state = right_update(1, shift_e_in[...])
            right_out[...] = value
    for o in range(4):
        pltpu.make_async_copy(rel_in.at[o], rel_in.at[o], rel_r.at[o]).wait()
    rel_sum[sub] = sum(rel_in[o].astype(F32) for o in range(4)).astype(BF16)
    shares = [
        remote(rel_sum.at[sub], rel_sum.at[sub], sum_s.at[0], sum_r.at[0], relatives[0]),
        remote(rel_sum.at[sub], rel_sum.at[sub], sum_s.at[1], sum_r.at[1], relatives[1]),
        remote(rel_sum.at[relatives[1][1]], rel_sum.at[relatives[1][1]], sum_s.at[2], sum_r.at[2], relatives[0]),
    ]
    shares[1].start()
    shares[0].start()
    rel_out[sub] = rel_sum[sub].astype(F32)
    shares[1].wait_recv()
    shares[2].start()
    rel_out[relatives[1][1]] = rel_sum[relatives[1][1]].astype(F32)
    shares[0].wait_recv()
    rel_out[relatives[0][1]] = rel_sum[relatives[0][1]].astype(F32)
    shares[2].wait_recv()
    rel_out[relatives[2][1]] = rel_sum[relatives[2][1]].astype(F32)
    for copy in shares:
        copy.wait_send()
    for o in range(4):
        stays = (core == 0) & (sub == o)
        pl.when(jnp.logical_not(stays))(
            remote(rel_send.at[o], rel_in.at[sub], rel_s.at[o], rel_r.at[sub], (home, o)).wait_send)
    for copy in shifts:
        copy.wait_send()
    sent(7)


def per_device(left_emb, left_state, right_emb, right_state, rel_ops, left_ids, right_ids, relations, negatives, live):
    vmem = pltpu.VMEM
    dma = pltpu.SemaphoreType.DMA
    whole = pl.BlockSpec(memory_space=pltpu.VMEM)
    return pl.pallas_call(
        kernel,
        out_shape=(
            jax.ShapeDtypeStruct((ROWS, WIDTH), F32),
            jax.ShapeDtypeStruct((PART, WIDTH), F32),
            jax.ShapeDtypeStruct((4, WIDTH, WIDTH), F32),
        ),
        in_specs=[pl.BlockSpec(memory_space=pl.ANY)] * 10,
        out_specs=[whole] * 3,
        scratch_shapes=[
            vmem((ROWS, WIDTH), F32),
            vmem((1, ROWS), F32),
            vmem((PART, WIDTH), F32),
            vmem((1, PART), F32),
            vmem((4, WIDTH, WIDTH), BF16),
            vmem((2, EDGES), jnp.int32),
            vmem((2, EDGES), jnp.int32),
            vmem((2, 1, EDGES), jnp.int32),
            vmem((2, 2, NEG), jnp.int32),
            vmem((1, 2), jnp.int32),
            vmem((2, DOM, 16, 128), BF16),
            vmem((8, DOM, 16, 128), BF16),
            vmem((2, 4, 256, EDGES), BF16),
            vmem((2, 4, EDGES, 256), BF16),
            vmem((2, 4, ROWS, 256), BF16),
            vmem((2, 4, 256, ROWS), BF16),
            vmem((EDGES, 8), F32),
            vmem((8, BLOCK), F32),
            vmem((4, WIDTH, WIDTH), BF16),
            vmem((2, 4, 256, WIDTH), BF16),
            vmem((EDGES, WIDTH), F32),
            vmem((EDGES, WIDTH), BF16),
            vmem((EDGES, WIDTH), BF16),
            vmem((EDGES, BLOCK), BF16),
            vmem((2, 4, PART, WIDTH), BF16),
            vmem((2, 2, 2, PART, WIDTH), BF16),
            vmem((2, 2, PART, WIDTH), BF16),
            vmem((2, PART, WIDTH), BF16),
            vmem((2, PART, WIDTH), BF16),
            vmem((ROWS, 1), F32),
            vmem((PART, 1), F32),
            vmem((PART, WIDTH), BF16),
            vmem((PART, WIDTH), BF16),
            vmem((8, PART), F32),
            vmem((8, PART), F32),
            vmem((4, WIDTH, WIDTH), F32),
            vmem((4, WIDTH, WIDTH), BF16),
            vmem((4, WIDTH, WIDTH), BF16),
            vmem((4, WIDTH, WIDTH), BF16),
            dma((8,)), dma((8, 4)), dma((2, 3)), dma((2, 3)), dma((2, 2)), dma((2, 2)),
            dma((2,)), dma((2,)), dma((4,)), dma((4,)), dma((3,)), dma((3,)), dma, dma, dma((10,)),
        ],
        compiler_params=pltpu.CompilerParams(collective_id=0, has_side_effects=True, vmem_limit_bytes=56 << 20),
    )(
        left_emb, left_state.reshape(1, -1), right_emb, right_state.reshape(1, -1), rel_ops, left_ids, right_ids,
        jnp.swapaxes(relations, 1, 2), negatives, live.T,
    )


def solution(mesh):
    placed = (
        P(("dom", "sub"), None),
        P(("dom", "sub")),
        P(("dom", "sub"), None),
        P(("dom", "sub")),
        P("dom", None, None),
        P(None, ("dom", "sub")),
        P(None, ("dom", "sub")),
        P(None, ("dom", "sub"), None),
        P(None, ("dom", "sub"), None),
        P(None, ("dom", "sub")),
    )
    return jax.shard_map(
        per_device,
        mesh=mesh,
        in_specs=placed,
        out_specs=(P(("dom", "sub"), None), P(("dom", "sub"), None), P("dom", None, None)),
        check_vma=False,
    )
```

```python
import jax
import jax.numpy as jnp
from jax import lax
from jax.experimental import pallas as pl
from jax.experimental.pallas import tpu as pltpu
from jax.sharding import PartitionSpec as P

LEARNING_RATE = 0.1
STABILIZER = 1e-06
MESH = pl.DeviceIdType.MESH
F32 = jnp.float32
BF16 = jnp.bfloat16
NX, NY, NZ = 4, 4, 8
DOM = NX * NY * NZ
WIDTH = 256
EDGES = 512
SLOTS = 1024
ROWS = 512
BLOCK = 1024
PART = 256
NEG = 1024


def dot(a, b):
    return lax.dot_general(a, b, (((1,), (0,)), ((), ())), preferred_element_type=F32)


def dot_bt(a, b):
    return lax.dot_general(a, b, (((1,), (1,)), ((), ())), preferred_element_type=F32)


def dot_at(a, b):
    return lax.dot_general(a, b, (((0,), (0,)), ((), ())), preferred_element_type=F32)


def iota(shape, dim):
    return lax.broadcasted_iota(jnp.int32, shape, dim)


def onehot(hit):
    return jnp.where(hit, 1.0, 0.0).astype(BF16)


def pack(rows):
    n = rows.shape[0] // 8
    low = rows[:, :128].reshape(n, 8, 128)
    high = rows[:, 128:].reshape(n, 8, 128)
    return jnp.concatenate([low, high], axis=1).astype(BF16)


def unpack(chunks):
    n = chunks.shape[0]
    wide = chunks.astype(F32)
    low = wide[:, :8].reshape(n * 8, 128)
    high = wide[:, 8:].reshape(n * 8, 128)
    return jnp.concatenate([low, high], axis=1)


def place():
    me = lax.axis_index("dom")
    sub = lax.axis_index("sub")
    return me // (NY * NZ), (me // NZ) % NY, me % NZ, sub // 2, sub % 2


ALONG_Z = ((0, 0), (0, 1), (1, 0), (1, 1), (7, 0), (7, 1), (2, 0), (6, 0))
BACKWARD = (0, 1, 4, 5, 2, 3, 7, 6)


def each_partner(sign, dx, visit):
    mx, my, mz, yh, core = place()
    mine = (mx * NY + my) * NZ
    qx = lax.rem(mx + (dx if sign > 0 else NX - dx), NX)
    for dy in range(NY):
        qy = lax.rem(my + dy, NY)
        if dy == 0:
            flips = (0, 0)
        elif dy == 1:
            flips = (jnp.where(my == NY - 1, 1, 0),) * 2
        elif dy == NY - 1:
            flips = (jnp.where(my == 0, 1, 0),) * 2
        else:
            flips = (core, lax.rem(mx + qx, 2))
        base = (qx * NY + qy) * NZ
        for j, (dz, other_core) in enumerate(ALONG_Z):
            z = lax.rem(mz + dz, NZ)
            there = 1 - core if other_core else core
            sub = lax.rem(yh + flips[other_core], 2) * 2 + there
            owner = base + lax.rem(z + 4 * there, NZ)
            visit(owner, base + j, mine + BACKWARD[j], (base + z, sub), dy == 0 and j == 0)


def kernel(
    left_hbm, lstate_hbm, right_hbm, rstate_hbm, rel_hbm, lids_hbm, rids_hbm, rels_hbm, negs_hbm, live_hbm,
    left_out, right_out, rel_out,
    left_now, lstate_ref, right_now, rstate_ref, rel_now, lids_ref, rids_ref, rels_ref, negs_ref, live_ref,
    send, recv, to_slot, from_slot, row_slot, slot_row, ids, counts, rel_t, inbox, total, moved, edge_grad, weights,
    blk, part, part_in, half, half_in, lstate, rstate, shift_e, shift_e_in, shift_s, shift_s_in, rel_acc, rel_send, rel_in, rel_sum,
    a2a_s, a2a_r, gat_s, gat_r, red_s, red_r, shf_s, shf_r, rel_s, rel_r, sum_s, sum_r, swp_s, swp_r, load_s,
):
    me = lax.axis_index("dom")
    sub = lax.axis_index("sub")
    mx, my, mz, yh, core = place()
    across_z = (mx * NY + my) * NZ + lax.rem(mz + 4, NZ)
    home = jnp.where(core == 0, me, across_z)
    following = (lax.rem(me + 1, DOM), sub)
    previous = (lax.rem(me + DOM - 1, DOM), sub)
    relatives = [(me, lax.rem(sub // 2 + o // 2, 2) * 2 + lax.rem(core + o % 2, 2)) for o in (1, 2, 3)]

    sources = (left_hbm, lstate_hbm, right_hbm, rstate_hbm, rel_hbm, lids_hbm, rids_hbm, rels_hbm, negs_hbm, live_hbm)
    places = (left_now, lstate_ref, right_now, rstate_ref, rel_now, lids_ref, rids_ref, rels_ref, negs_ref, live_ref)
    copies = [pltpu.make_async_copy(src, dst, load_s.at[i]) for i, (src, dst) in enumerate(zip(sources, places))]
    for i in (7, 5, 6, 1, 3, 9, 0, 2, 8):
        copies[i].start()
    barrier = pltpu.get_barrier_semaphore()

    def greet(device):
        pl.semaphore_signal(barrier, inc=1, device_id=device, device_id_type=MESH)

    def planes(body):
        def step(dx, carry):
            body(dx)
            return carry

        lax.fori_loop(0, NX, step, 0)

    def unrolled(body):
        for dx in range(NX):
            body(dx)

    def greet_plane(dx):
        def visit(owner, other, there, device, first):
            if first:
                pl.when(dx != 0)(lambda: greet(device))
            else:
                greet(device)

        each_partner(1, dx, visit)

    planes(greet_plane)
    for device in relatives + [following, previous] + [(across_z, o) for o in range(4)]:
        greet(device)

    def remote(src, dst, send_sem, recv_sem, device):
        return pltpu.make_async_remote_copy(
            src_ref=src, dst_ref=dst, send_sem=send_sem, recv_sem=recv_sem, device_id=device, device_id_type=MESH
        )

    def blocks(count, body):
        def step(i, carry):
            body(i)
            return carry

        lax.fori_loop(0, count, step, 0)

    def plane_at(sign, dx):
        return lax.rem(mx + (dx if sign > 0 else NX - dx), NX)

    def send_plane(k, dx):
        outward = k % 2 == 0

        def visit(owner, other, there, device, first):
            chunk, landing = (owner, there) if outward else (other, home)
            copy = remote(send.at[k % 2, chunk], recv.at[k, landing], a2a_s.at[k], a2a_r.at[k, dx], device)
            if first:
                if dx == 0:
                    pltpu.make_async_copy(send.at[k % 2, chunk], recv.at[k, landing], a2a_r.at[k, dx]).start()
                else:
                    copy.start()
            else:
                copy.start()

        each_partner(1 if outward else -1, dx, visit)

    def sent(k):
        most = send.at[k % 2, pl.ds(0, DOM - 1)]
        pltpu.make_async_copy(most, most, a2a_s.at[k]).wait()

    def arrived(k, dx):
        plane = recv.at[k, pl.ds(0, 32)]
        pltpu.make_async_copy(plane, plane, a2a_r.at[k, dx]).wait()
        return plane_at(-1 if k % 2 == 0 else 1, dx)

    for i in (1, 3, 5, 6, 7, 9):
        copies[i].wait()
    loads = [copies[i] for i in (0, 2, 8)]
    rows = jnp.concatenate(
        [rels_ref[0].astype(F32), rels_ref[1].astype(F32), lids_ref[...].astype(F32), rids_ref[...].astype(F32), lstate_ref[...],
         jnp.zeros((1, EDGES), F32)], axis=0)
    ids[...] = jnp.transpose(rows)
    lstate[...] = ids[:, 6:7]
    rstate[...] = jnp.transpose(jnp.broadcast_to(rstate_ref[...], (8, PART)))[:, 0:1]

    def index_work(r, stage):
        if stage == 0:
            rel_row = rels_ref[r].astype(F32)
            rel_col = ids[:, r : r + 1]
            same = rel_row == rel_col
            lane, line = iota((EDGES, EDGES), 1), iota((EDGES, EDGES), 0)
            row_rank = jnp.sum(jnp.where(same & (line < lane), 1.0, 0.0), axis=0, keepdims=True)
            col_rank = jnp.sum(jnp.where(same & (lane < line), 1.0, 0.0), axis=1, keepdims=True)
            ids[:, 7:8] = 2.0 * rel_col + col_rank
            row_ids = (2.0 * rel_row + row_rank).astype(jnp.int32)
            gather = onehot(iota((EDGES, ROWS), 1) == ids[:, 2 + r : 3 + r].astype(jnp.int32))

            def fill(i):
                place_of = onehot(iota((256, EDGES), 0) + i * 256 == row_ids)
                to_slot[r, i] = place_of
                slot_row[r, i] = dot(place_of, gather).astype(BF16)

            blocks(4, fill)
        else:
            slot = ids[:, 7:8].astype(jnp.int32)
            for i in range(4):
                from_slot[r, i] = onehot(iota((EDGES, 256), 1) + i * 256 == slot)
            scatter = onehot(iota((ROWS, EDGES), 0) == lids_ref[r : r + 1, :])
            for i in range(4):
                row_slot[r, i] = dot(scatter, from_slot[r, i]).astype(BF16)
            for c in range(2):
                named = negs_ref[r, c : c + 1, :]
                high = onehot(iota((16, NEG), 0) == named // 128)
                low = onehot(iota((128, NEG), 0) == named % 128)
                tally = dot_bt(high, low)
                counts[2 * r + c : 2 * r + c + 1, :] = (
                    jnp.concatenate([tally[i : i + 1, :] for i in range(8)], axis=1) * (1.0 / NEG))

    def send_rows(k, table, values):
        def step(dx):
            p = plane_at(1, dx)
            send[k % 2, pl.ds(p * 32, 32)] = pack(dot(table[p], values))
            send_plane(k, dx)

        unrolled(step)

    def keep(o):
        return (iota((256, WIDTH), 0) % 8) // 2 == o

    def adagrad(value, state, gradient):
        state = state + jnp.mean(gradient * gradient, axis=1, keepdims=True)
        return value - LEARNING_RATE / (jnp.sqrt(state) + STABILIZER) * gradient, state

    def block_copies(r):
        theirs = relatives[1][1]
        return [
            remote(blk.at[r, sub], blk.at[r, sub], gat_s.at[r, 0], gat_r.at[r, 0], relatives[0]),
            remote(blk.at[r, sub], blk.at[r, sub], gat_s.at[r, 1], gat_r.at[r, 1], relatives[1]),
            remote(blk.at[r, theirs], blk.at[r, theirs], gat_s.at[r, 2], gat_r.at[r, 2], relatives[0]),
        ]

    def gather_block(r):
        copies = block_copies(r)
        copies[1].start()
        copies[0].start()

    def pass_block_on(r):
        copies = block_copies(r)
        copies[1].wait_recv()
        copies[2].start()

    def block_ready(r):
        copies = block_copies(r)
        copies[0].wait()
        copies[1].wait_send()
        copies[2].wait()

    def sum_copies(r):
        return [
            remote(part.at[r, 1 - core], part_in.at[r], red_s.at[r, 0], red_r.at[r, 0], relatives[0]),
            remote(half.at[r], half_in.at[r], red_s.at[r, 1], red_r.at[r, 1], relatives[1]),
        ]

    def sum_across(r):
        copies = sum_copies(r)
        copies[0].wait()
        half[r] = (part[r, core, 1 - yh].astype(F32) + part_in[r, 1 - yh].astype(F32)).astype(BF16)
        copies[1].start()

    def right_update(r, value):
        sum_copies(r)[1].wait()
        gradient = part[r, core, yh].astype(F32) + part_in[r, yh].astype(F32) + half_in[r].astype(F32)
        return adagrad(value.astype(F32), rstate[...], gradient)

    index_work(0, 0)
    for copy in loads:
        copy.wait()
    left_bf = left_now[...].astype(BF16)
    blk[0, sub] = right_now[...].astype(BF16)
    pl.semaphore_wait(barrier, DOM - 1 + 9)
    swap = remote(rel_hbm, rel_now, swp_s, swp_r, (across_z, sub))
    pl.when(core == 1)(swap.start)
    pl.when(core == 0)(copies[4].start)
    rel_acc[...] = jnp.zeros((4, WIDTH, WIDTH), F32)

    for r in range(2):
        k = 4 * r
        send_rows(k, slot_row.at[r], left_bf)
        total[...] = jnp.zeros((EDGES, WIDTH), F32)
        if r == 0:
            gather_block(0)
            index_work(0, 1)
            pl.when(core == 1)(swap.wait)
            pl.when(core == 0)(copies[4].wait)
        else:
            value, state = right_update(0, right_now[...])
            shift_e[...] = value.astype(BF16)
            shift_s[...] = jnp.transpose(jnp.broadcast_to(state, (PART, 128)))[0:8, :]
            shifts = [
                remote(shift_e, shift_e_in, shf_s.at[0], shf_r.at[0], following),
                remote(shift_s, shift_s_in, shf_s.at[1], shf_r.at[1], following),
            ]
            for copy in shifts:
                copy.start()
            sent(k - 1)

        def forward(dx):
            p = arrived(k, dx)
            row = unpack(recv[k, pl.ds(p * 32, 32)])
            inbox[r, p] = row.astype(BF16)
            mapped = sum(dot(jnp.where(keep(o), row, 0.0).astype(BF16), rel_now[o]) for o in range(4))
            send[(k + 1) % 2, pl.ds(p * 32, 32)] = pack(mapped)
            send_plane(k + 1, dx)

        unrolled(forward)
        if r == 0:
            for o in range(4):
                rel_t[o] = jnp.transpose(rel_now[o].astype(F32)).astype(BF16)
            index_work(1, 0)
            index_work(1, 1)
        else:
            for copy in shifts:
                copy.wait_recv()
            blk[1, sub] = shift_e_in[...]
            gather_block(1)
            rstate[...] = jnp.transpose(shift_s_in[...])[:, 0:1]
        if r == 0:
            pass_block_on(r)

        def settle(dx):
            if r == 1:
                pl.when(dx == NX - 1)(lambda: pass_block_on(1))
            p = arrived(k + 1, dx)
            total[...] += dot(from_slot[r, p], unpack(recv[k + 1, pl.ds(p * 32, 32)]).astype(BF16))

        planes(settle)
        moved[...] = total[...].astype(BF16)
        total[...] = jnp.zeros((EDGES, WIDTH), F32)
        block_ready(r)

        live = live_ref[:, r : r + 1]

        def score(i):
            at = pl.ds(i * 128, 128)
            y = moved[at, :]
            scores = jnp.concatenate([dot_bt(y, blk[r, j]) for j in range(4)], axis=1)
            mask = jnp.where(iota((128, 1), 0) + i * 128 < live, 1.0, 0.0)
            named = iota((128, BLOCK), 1) == ids[at, 4 + r : 5 + r].astype(jnp.int32)
            positive = jnp.sum(jnp.where(named, scores, 0.0), axis=1, keepdims=True)
            pull = -jax.nn.sigmoid(-positive) * mask
            push = jax.nn.sigmoid(scores) * counts[pl.ds(2 * r + i // 2, 1), :] * mask
            weight = (push + jnp.where(named, pull, 0.0)).astype(BF16)
            weights[at, :] = weight
            grad = sum(dot(weight[:, j * 256 : (j + 1) * 256], blk[r, j]) for j in range(4))
            edge_grad[at, :] = grad.astype(BF16)

        blocks(4, score)
        sent(k)
        send_rows(k + 2, to_slot.at[r], edge_grad[...])
        for j in range(4):
            part[r, j % 2, j // 2] = dot_at(weights[:, j * 256 : (j + 1) * 256], moved[...]).astype(BF16)
        sum_copies(r)[0].start()
        sent(k + 1)

        def backward(dx):
            if dx == 1:
                sum_across(r)
            p = arrived(k + 2, dx)
            row = unpack(recv[k + 2, pl.ds(p * 32, 32)])
            kept = [jnp.where(keep(o), row, 0.0).astype(BF16) for o in range(4)]
            send[(k + 3) % 2, pl.ds(p * 32, 32)] = pack(sum(dot(kept[o], rel_t[o]) for o in range(4)))
            send_plane(k + 3, dx)
            for o in range(4):
                rel_acc[o] += dot_at(inbox[r, p], kept[o])

        unrolled(backward)
        if r == 1:
            for o in range(4):
                rel_send[o] = rel_acc[o].astype(BF16)
                stays = (core == 0) & (sub == o)
                pl.when(stays)(pltpu.make_async_copy(rel_send.at[o], rel_in.at[sub], rel_r.at[sub]).start)
                pl.when(jnp.logical_not(stays))(
                    remote(rel_send.at[o], rel_in.at[sub], rel_s.at[o], rel_r.at[sub], (home, o)).start)

        def settle_back(dx):
            p = arrived(k + 3, dx)
            total[...] += dot(row_slot[r, p], unpack(recv[k + 3, pl.ds(p * 32, 32)]).astype(BF16))

        planes(settle_back)
        sent(k + 2)
        value, state = adagrad(left_now[...], lstate[...], total[...])
        if r == 0:
            left_now[...] = value
            lstate[...] = state
            left_bf = value.astype(BF16)
        else:
            left_out[...] = value
            value, state = right_update(1, shift_e_in[...])
            right_out[...] = value
    for o in range(4):
        pltpu.make_async_copy(rel_in.at[o], rel_in.at[o], rel_r.at[o]).wait()
    rel_sum[sub] = sum(rel_in[o].astype(F32) for o in range(4)).astype(BF16)
    shares = [
        remote(rel_sum.at[sub], rel_sum.at[sub], sum_s.at[0], sum_r.at[0], relatives[0]),
        remote(rel_sum.at[sub], rel_sum.at[sub], sum_s.at[1], sum_r.at[1], relatives[1]),
        remote(rel_sum.at[relatives[1][1]], rel_sum.at[relatives[1][1]], sum_s.at[2], sum_r.at[2], relatives[0]),
    ]
    shares[1].start()
    shares[0].start()
    rel_out[sub] = rel_sum[sub]
    shares[1].wait_recv()
    shares[2].start()
    rel_out[relatives[1][1]] = rel_sum[relatives[1][1]]
    shares[0].wait_recv()
    rel_out[relatives[0][1]] = rel_sum[relatives[0][1]]
    shares[2].wait_recv()
    rel_out[relatives[2][1]] = rel_sum[relatives[2][1]]
    for copy in shares:
        copy.wait_send()
    for o in range(4):
        stays = (core == 0) & (sub == o)
        pl.when(jnp.logical_not(stays))(
            remote(rel_send.at[o], rel_in.at[sub], rel_s.at[o], rel_r.at[sub], (home, o)).wait_send)
    for copy in shifts:
        copy.wait_send()
    sent(7)


def place_results(left, right, rel, left_out, right_out, rel_out):
    left_out[...] = left[...]
    right_out[...] = right[...]
    rel_out[...] = rel[...].astype(F32)


def per_device(left_emb, left_state, right_emb, right_state, rel_ops, left_ids, right_ids, relations, negatives, live):
    vmem = pltpu.VMEM
    dma = pltpu.SemaphoreType.DMA
    whole = pl.BlockSpec(memory_space=pltpu.VMEM)
    def shapes(rel_type):
        return (
            jax.ShapeDtypeStruct((ROWS, WIDTH), F32),
            jax.ShapeDtypeStruct((PART, WIDTH), F32),
            jax.ShapeDtypeStruct((4, WIDTH, WIDTH), rel_type),
        )

    results = pl.pallas_call(
        kernel,
        out_shape=shapes(BF16),
        in_specs=[pl.BlockSpec(memory_space=pl.ANY)] * 10,
        out_specs=[whole] * 3,
        scratch_shapes=[
            vmem((ROWS, WIDTH), F32),
            vmem((1, ROWS), F32),
            vmem((PART, WIDTH), F32),
            vmem((1, PART), F32),
            vmem((4, WIDTH, WIDTH), BF16),
            vmem((2, EDGES), jnp.int32),
            vmem((2, EDGES), jnp.int32),
            vmem((2, 1, EDGES), jnp.int32),
            vmem((2, 2, NEG), jnp.int32),
            vmem((1, 2), jnp.int32),
            vmem((2, DOM, 16, 128), BF16),
            vmem((8, DOM, 16, 128), BF16),
            vmem((2, 4, 256, EDGES), BF16),
            vmem((2, 4, EDGES, 256), BF16),
            vmem((2, 4, ROWS, 256), BF16),
            vmem((2, 4, 256, ROWS), BF16),
            vmem((EDGES, 8), F32),
            vmem((8, BLOCK), F32),
            vmem((4, WIDTH, WIDTH), BF16),
            vmem((2, 4, 256, WIDTH), BF16),
            vmem((EDGES, WIDTH), F32),
            vmem((EDGES, WIDTH), BF16),
            vmem((EDGES, WIDTH), BF16),
            vmem((EDGES, BLOCK), BF16),
            vmem((2, 4, PART, WIDTH), BF16),
            vmem((2, 2, 2, PART, WIDTH), BF16),
            vmem((2, 2, PART, WIDTH), BF16),
            vmem((2, PART, WIDTH), BF16),
            vmem((2, PART, WIDTH), BF16),
            vmem((ROWS, 1), F32),
            vmem((PART, 1), F32),
            vmem((PART, WIDTH), BF16),
            vmem((PART, WIDTH), BF16),
            vmem((8, PART), F32),
            vmem((8, PART), F32),
            vmem((4, WIDTH, WIDTH), F32),
            vmem((4, WIDTH, WIDTH), BF16),
            vmem((4, WIDTH, WIDTH), BF16),
            vmem((4, WIDTH, WIDTH), BF16),
            dma((8,)), dma((8, 4)), dma((2, 3)), dma((2, 3)), dma((2, 2)), dma((2, 2)),
            dma((2,)), dma((2,)), dma((4,)), dma((4,)), dma((3,)), dma((3,)), dma, dma, dma((10,)),
        ],
        compiler_params=pltpu.CompilerParams(collective_id=0, has_side_effects=True, vmem_limit_bytes=56 << 20),
    )(
        left_emb, left_state.reshape(1, -1), right_emb, right_state.reshape(1, -1), rel_ops, left_ids, right_ids,
        jnp.swapaxes(relations, 1, 2), negatives, live.T,
    )
    return pl.pallas_call(
        place_results,
        out_shape=shapes(F32),
        in_specs=[whole] * 3,
        out_specs=[whole] * 3,
    )(*results)


def solution(mesh):
    placed = (
        P(("dom", "sub"), None),
        P(("dom", "sub")),
        P(("dom", "sub"), None),
        P(("dom", "sub")),
        P("dom", None, None),
        P(None, ("dom", "sub")),
        P(None, ("dom", "sub")),
        P(None, ("dom", "sub"), None),
        P(None, ("dom", "sub"), None),
        P(None, ("dom", "sub")),
    )
    return jax.shard_map(
        per_device,
        mesh=mesh,
        in_specs=placed,
        out_specs=(P(("dom", "sub"), None), P(("dom", "sub"), None), P("dom", None, None)),
        check_vma=False,
    )
```
